512 devices in a mesh: gz: 32 (over z_lo, y), xy: 16 (over z_hi, x, core).
Axes of the slice: x: 4, y: 4, z: 16 (z_hi: 2, z_lo: 8; z = z_hi * 8 + z_lo), core: 2. Of those that a mesh axis runs over, the one named last changes fastest.
Arguments:
- up_source: bfloat16 [32, 2, 32, 4096], P('gz', None, None, 'xy'), may hold values from -6 to 6
- down_source: bfloat16 [32, 2, 32, 4096], P('gz', None, None, 'xy'), may hold values from -6 to 6
- source_layer: int32 [32], replicated, may hold values from 0 to 31, as said below
- u_factor: bfloat16 [32, 16, 16, 2, 128, 256], P('gz', 'xy'), may hold values from -0.078125 to 0.078125
- v_factor: bfloat16 [32, 16, 16, 2, 128, 256], P('gz', 'xy'), may hold values from -0.25 to 0.25
- block_rank: int32 [32, 16, 16], P('gz', 'xy'), may hold values from 1 to 4
Outputs:
- up_trace: bfloat16 [32, 2, 32, 4096], P('gz', None, None, 'xy')
- down_trace: bfloat16 [32, 2, 32, 4096], P('gz', None, None, 'xy')
The draws below stay inside these ranges and needn't reach their ends.
Inputs may be any that keep to these rules, and one draw needn't show every extreme that they name: `source_layer`: the index of the layer slab in which source s lies; source 0 lies in slab 0 and source 1 in slab 32 - 1. `block_rank`: block (i, j) of interface l has rank 32 times this number.
All inputs are finite; a program needn't handle non-finite values.
Results may differ from the reference program's by a relative error of at most 0.007.
Values may be sent and summed in bfloat16 or wider, within the bound.
No kernel may reach another device: no remote copies, remote signals or barrier semaphores. Data moves between devices by JAX's collectives and lax.ppermute only.
A program may use at most 64 MiB of HBM per device.

```python
import jax
import jax.numpy as jnp
from jax import lax

BLK = 256
RMAX = 128
SRC = 32
STEPS = 3
LAYERS = 32
N = 4096
NB = 16
RANK_STEP = 32


def draw_source_layer(key, part):
    drawn = jax.random.randint(key, (SRC,), 0, LAYERS, dtype=jnp.int32)
    position = jnp.arange(SRC, dtype=jnp.int32)
    drawn = jnp.where(position == 0, jnp.zeros_like(drawn), drawn)
    drawn = jnp.where(position == 1, jnp.full_like(drawn, LAYERS - 1), drawn)
    return drawn


def set_ends(result, stream_key, least, largest):
    longest = result.shape.index(max(result.shape))
    spots = []
    for shift in (0, 1):
        where = [jax.random.randint(jax.random.fold_in(stream_key, axis), (), 0, length) for axis, length in enumerate(result.shape)]
        where[longest] = (where[longest] + shift) % result.shape[longest]
        spots.append(tuple(where))
    return result.at[spots[0]].set(least).at[spots[1]].set(largest)


def shard_levels(own_key, shape, split, low, high):
    def one(dim, parts):
        draws = jax.random.uniform(jax.random.fold_in(jax.random.fold_in(own_key, 6), dim), (parts,), jnp.float32, low / len(split), high / len(split))
        return jnp.repeat(jnp.exp(draws), shape[dim] // parts).reshape((-1,) + (1,) * (len(shape) - dim - 1))

    level = one(*split[0])
    for cut in split[1:]:
        level = level * one(*cut)
    return level


def bell_draw(rng, dims, spread, most, shards=(), held_as=jnp.bfloat16):
    level = shard_levels(rng, dims, shards, -0.22, 0.18) if shards else 1.0
    entries = jax.random.normal(rng, dims, jnp.float32) * spread * level
    return jnp.minimum(jnp.maximum(entries, -most), most).astype(held_as)


def setup_inputs(seed: int = 0) -> dict:
    key_of = jax.random.split(jax.random.key(seed), 7)
    up_source = bell_draw(key_of[0], (LAYERS, 2, SRC, N), 1.0, 6.0, ((0, 32), (3, 16)))
    down_source = bell_draw(key_of[1], (LAYERS, 2, SRC, N), 1.0, 6.0, ((0, 32), (3, 16)))
    source_layer = draw_source_layer(jax.random.fold_in(key_of[6], 71), 0)
    u_factor = bell_draw(key_of[3], (LAYERS, NB, NB, 2, RMAX, BLK), (3 * NB * RMAX) ** -0.5, 0.078125, ((0, 32), (1, 16)))
    v_factor = bell_draw(key_of[4], (LAYERS, NB, NB, 2, RMAX, BLK), (2 * BLK) ** -0.5, 0.25, ((0, 32), (1, 16)))
    block_rank = set_ends(jax.random.randint(key_of[5], (LAYERS, NB, NB), 1, 5), jax.random.fold_in(key_of[5], 1), 1, 4).astype(jnp.int32)
    return dict(up_source=up_source, down_source=down_source, source_layer=source_layer, u_factor=u_factor, v_factor=v_factor, block_rank=block_rank)


def complex_parts(product):
    real = product[..., 0, :, 0, :] - product[..., 1, :, 1, :]
    imag = product[..., 0, :, 1, :] + product[..., 1, :, 0, :]
    return jnp.stack([real, imag], axis=-3)


def round_half(values):
    return lax.optimization_barrier(values.astype(jnp.bfloat16)).astype(jnp.float32)


def layer_apply(u_layer, v_layer, rank_layer, up_layer, above_layer):
    keep_rank = jnp.arange(RMAX, dtype=jnp.int32)[None, None, :] < RANK_STEP * rank_layer[:, :, None]
    u_float = u_layer.astype(jnp.float32)
    v_float = v_layer.astype(jnp.float32)
    pieces = up_layer.astype(jnp.float32).reshape(2, SRC, NB, BLK)
    up_coef = complex_parts(jnp.einsum('asjb,ijcrb->ijascr', pieces, v_float))
    up_coef = round_half(jnp.where(keep_rank[:, :, None, None, :], up_coef, 0.0))
    forward = complex_parts(jnp.einsum('ijasr,ijcrb->iascb', up_coef, u_float))
    forward = jnp.transpose(forward, (1, 2, 0, 3)).reshape(2, SRC, N)
    upper = above_layer.astype(jnp.float32).reshape(2, SRC, NB, BLK)
    down_coef = complex_parts(jnp.einsum('asib,ijcrb->ijascr', upper, u_float))
    down_coef = round_half(jnp.where(keep_rank[:, :, None, None, :], down_coef, 0.0))
    backward = complex_parts(jnp.einsum('ijasr,ijcrb->jascb', down_coef, v_float))
    backward = jnp.transpose(backward, (1, 2, 0, 3)).reshape(2, SRC, N)
    return forward, backward


def reference(up_source, down_source, source_layer, u_factor, v_factor, block_rank):
    layer_ids = jnp.arange(LAYERS, dtype=jnp.int32)
    up_mask = (layer_ids[:, None] >= source_layer[None, :])[:, None, :, None]
    down_mask = (layer_ids[:, None] <= source_layer[None, :])[:, None, :, None]
    active_up = jnp.where(up_mask, up_source, jnp.zeros_like(up_source))
    active_down = jnp.where(down_mask, down_source, jnp.zeros_like(down_source))
    up_trace = active_up
    down_trace = active_down
    for sweep_index in range(STEPS):
        upper = jnp.concatenate([down_trace[1:], jnp.zeros_like(down_trace[:1])], axis=0)
        forward, backward = lax.map(lambda items: layer_apply(*items), (u_factor, v_factor, block_rank, up_trace, upper))
        lower = jnp.concatenate([jnp.zeros_like(forward[:1]), forward[:-1]], axis=0)
        up_trace = (active_up.astype(jnp.float32) + lower).astype(jnp.bfloat16)
        down_trace = (active_down.astype(jnp.float32) + backward).astype(jnp.bfloat16)
    return up_trace, down_trace
```

```python
import functools

import jax
import jax.numpy as jnp
from jax import lax
from jax.experimental import pallas as pl
from jax.experimental.pallas import tpu as pltpu
from jax.sharding import PartitionSpec as P

STEPS = 3
XS = 4
PAIR = 2
ROWS = 64
HALF = 32
BF = jnp.bfloat16
F32 = jnp.float32


def dot_rows(a, b):
    return lax.dot_general(a, b, (((1,), (1,)), ((), ())), preferred_element_type=F32)


def dot_cols(a, b):
    return lax.dot_general(a, b, (((1,), (0,)), ((), ())), preferred_element_type=F32)


def coefficients(product, limit):
    rank = product.shape[1] // 2
    real = product[:HALF, :rank] - product[HALF:, rank:]
    imag = product[:HALF, rank:] + product[HALF:, :rank]
    keep = lax.broadcasted_iota(jnp.int32, real.shape, 1) < limit
    real = jnp.where(keep, real, 0.0).astype(BF)
    imag = jnp.where(keep, imag, 0.0).astype(BF)
    top = jnp.concatenate([real, -imag], axis=1)
    bottom = jnp.concatenate([imag, real], axis=1)
    return jnp.concatenate([top, bottom], axis=0)


def block_of(x, z, c):
    return z * 8 + x * 2 + c


def spread_kernel(where_ref, rank_ref, hop_ref, far_ref, own0_ref, far0_ref, next_ref, u0_ref, v0_ref, u1_ref, v1_ref, out_ref):
    core = where_ref[0]
    z_own = where_ref[1]
    first_layer = where_ref[2] == 0

    @pl.when(core == 0)
    def _():
        for c in range(PAIR):
            own = jnp.where(first_layer, own0_ref[c], hop_ref[c])
            far = jnp.where(first_layer, far0_ref[c], far_ref[c])
            for z in range(2):
                block = jnp.where(z_own == z, own, far)
                for x in range(XS):
                    out_ref[x, z * PAIR + c] = block

    @pl.when(core == 1)
    def _():
        traces = []
        for c in range(PAIR):
            total = next_ref[c].astype(F32) + (hop_ref[c].astype(F32) + far_ref[c].astype(F32))
            traces.append(total.astype(BF))
        factors = ((1, u0_ref, v0_ref), (0, u1_ref, v1_ref))
        for x in range(XS):
            for z in range(2):
                for c in range(PAIR):
                    j = block_of(x, z, c)
                    total = None
                    for row, u_ref, v_ref in factors:
                        product = dot_rows(traces[row], u_ref[j])
                        coef = coefficients(product, rank_ref[row, j])
                        part = dot_cols(coef, v_ref[j])
                        total = part if total is None else total + part
                    out_ref[x, z * PAIR + c] = total.astype(BF)


def gather_kernel(where_ref, rank_ref, got_ref, next_ref, u0_ref, v0_ref, u1_ref, v1_ref, hop_ref, far_ref):
    core = where_ref[0]
    z_own = where_ref[1]

    @pl.when(core == 0)
    def _():
        factors = ((0, u0_ref, v0_ref), (1, u1_ref, v1_ref))
        for row, u_ref, v_ref in factors:
            total = next_ref[row].astype(F32)
            for x in range(XS):
                for z in range(2):
                    for c in range(PAIR):
                        j = block_of(x, z, c)
                        product = dot_rows(got_ref[x, z * PAIR + c], v_ref[j])
                        coef = coefficients(product, rank_ref[row, j])
                        total = total + dot_cols(coef, u_ref[j])
            block = total.astype(BF)
            hop_ref[row] = block
            far_ref[row] = block

    @pl.when(core == 1)
    def _():
        for c in range(PAIR):
            sums = []
            for z in range(2):
                total = got_ref[0, z * PAIR + c].astype(F32)
                for x in range(1, XS):
                    total = total + got_ref[x, z * PAIR + c].astype(F32)
                sums.append(total.astype(BF))
            hop_ref[c] = jnp.where(z_own == 0, sums[0], sums[1])
            far_ref[c] = jnp.where(z_own == 0, sums[1], sums[0])


def call(kernel, outs, scalars, arrays):
    smem = pl.BlockSpec(memory_space=pltpu.SMEM)
    vmem = pl.BlockSpec(memory_space=pltpu.VMEM)
    return pl.pallas_call(
        kernel,
        out_shape=outs,
        in_specs=[smem] * len(scalars) + [vmem] * len(arrays),
        out_specs=jax.tree.map(lambda _: vmem, outs),
        compiler_params=pltpu.CompilerParams(vmem_limit_bytes=48 * 1024 * 1024),
        cost_estimate=pl.CostEstimate(flops=64 * 2 * 64 * 256 * 256, bytes_accessed=10 * 1024 * 1024, transcendentals=0),
    )(*scalars, *arrays)


def on_device(layers, up_source, down_source, source_layer, u_factor, v_factor, block_rank):
    layer = lax.axis_index("gz")
    place = lax.axis_index("xy")
    core = place % 2
    z_own = place // 8
    both = ("gz", "xy")
    width = u_factor.shape[-1]
    max_rank = u_factor.shape[-2]
    step = max_rank // 4

    def send(block, target):
        route = []
        for l in range(layers):
            for i in range(16):
                to = target(l, i)
                if to is not None and 0 <= to[0] < layers:
                    route.append((l * 16 + i, to[0] * 16 + to[1]))
        return lax.ppermute(block, both, route)

    def ahead(l, i):
        return (l + 1, i) if i % 2 == 0 else (l - 1, i)

    def ahead_far(l, i):
        return (l + 1, i ^ 8) if i % 2 == 0 else (l - 1, i ^ 8)

    pairs = [[2 * k, 2 * k + 1] for k in range(8)]
    rings = [[block_of(x, z, c) for x in range(XS)] for z in range(2) for c in range(2)]

    up_mask = (layer >= source_layer)[None, :, None]
    down_mask = (layer <= source_layer)[None, :, None]
    active_up = jnp.where(up_mask, up_source[0], jnp.zeros_like(up_source[0])).reshape(ROWS, width)
    active_down = jnp.where(down_mask, down_source[0], jnp.zeros_like(down_source[0])).reshape(ROWS, width)
    ranks = block_rank[0, 0].astype(BF)
    rank_rows = jnp.broadcast_to(jnp.pad(ranks, (0, width - ranks.shape[0]))[None, :], (16, width))
    packed = jnp.concatenate([active_up, active_down, rank_rows], axis=0)
    chip = lax.all_gather(packed, "xy", axis=0, axis_index_groups=pairs)
    mine = jnp.where(core == 0, chip[:, :ROWS], chip[:, ROWS : 2 * ROWS])
    limits = (chip[:, 2 * ROWS, :16].astype(F32) * step).astype(jnp.int32)

    u_own = u_factor[0, 0].reshape(16, 2 * max_rank, width)
    v_own = v_factor[0, 0].reshape(16, 2 * max_rank, width)
    far0 = send(mine, lambda l, i: (l, i ^ 8) if i % 2 == 0 else None)
    following = send(mine, lambda l, i: (l - 1, i))
    u_other = lax.ppermute(u_own, "xy", [(i, i ^ 1) for i in range(16)])
    v_other = lax.ppermute(v_own, "xy", [(i, i ^ 1) for i in range(16)])

    where = jnp.stack([core, z_own, layer]).astype(jnp.int32)
    scalars = (where, limits)
    factors = (u_own, v_own, u_other, v_other)
    pair_shape = jax.ShapeDtypeStruct((PAIR, ROWS, width), BF)
    ring_shape = jax.ShapeDtypeStruct((XS, 2 * PAIR, ROWS, width), BF)

    hop = jnp.where(core == 0, mine, jnp.zeros_like(mine))
    far = far0
    for sweep in range(STEPS):
        sent = call(spread_kernel, ring_shape, scalars, (hop, far, mine, far0, following) + factors)
        got = lax.all_to_all(sent, "xy", 0, 0, axis_index_groups=rings)
        near, away = call(gather_kernel, (pair_shape, pair_shape), scalars, (got, following) + factors)
        if sweep < STEPS - 1:
            far = send(away, ahead_far)
            hop = send(near, ahead)

    last = send(away, lambda l, i: (l + 1, i) if i % 2 == 0 else (l, i ^ 8))
    up_pair = jnp.where(layer == 0, mine, last)
    down_pair = (mine.astype(F32) + (near.astype(F32) + last.astype(F32))).astype(BF)
    final = jnp.where(core == 0, up_pair, down_pair)
    swapped = lax.all_gather(final[1 - core], "xy", axis=0, axis_index_groups=pairs)
    kept = final[core]
    other = swapped[1 - core]
    up_trace = jnp.where(core == 0, kept, other).reshape(up_source.shape)
    down_trace = jnp.where(core == 0, other, kept).reshape(up_source.shape)
    return up_trace, down_trace


def solution(mesh):
    in_specs = (
        P("gz", None, None, "xy"),
        P("gz", None, None, "xy"),
        P(),
        P("gz", "xy", None, None, None, None),
        P("gz", "xy", None, None, None, None),
        P("gz", "xy", None),
    )
    out_specs = (P("gz", None, None, "xy"), P("gz", None, None, "xy"))
    return jax.shard_map(
        functools.partial(on_device, mesh.shape["gz"]),
        mesh=mesh,
        in_specs=in_specs,
        out_specs=out_specs,
        check_vma=False,
    )
```

```python
import functools

import jax
import jax.numpy as jnp
from jax import lax
from jax.experimental import pallas as pl
from jax.experimental.pallas import tpu as pltpu
from jax.sharding import PartitionSpec as P

STEPS = 3
XS = 4
PAIR = 2
ROWS = 64
HALF = 32
GROUPS = 4
LIMIT = 16 * 1024 * 1024
BF = jnp.bfloat16
F32 = jnp.float32


def dot_rows(a, b):
    return lax.dot_general(a, b, (((1,), (1,)), ((), ())), preferred_element_type=F32)


def dot_cols(a, b):
    return lax.dot_general(a, b, (((1,), (0,)), ((), ())), preferred_element_type=F32)


def coefficients(product, limit):
    rank = product.shape[1] // 2
    real = product[:HALF, :rank] - product[HALF:, rank:]
    imag = product[:HALF, rank:] + product[HALF:, :rank]
    keep = lax.broadcasted_iota(jnp.int32, real.shape, 1) < limit
    real = jnp.where(keep, real, 0.0).astype(BF)
    imag = jnp.where(keep, imag, 0.0).astype(BF)
    top = jnp.concatenate([real, -imag], axis=1)
    bottom = jnp.concatenate([imag, real], axis=1)
    return jnp.concatenate([top, bottom], axis=0)


def block_of(x, z, c):
    return z * 8 + x * 2 + c


def load_kernel(u0, v0, u1, v1, held_ref, sems):
    copies = [pltpu.make_async_copy(ref, held_ref.at[n], sems.at[n]) for n, ref in enumerate((u0, v0, u1, v1))]
    for copy in copies:
        copy.start()
    for copy in copies:
        copy.wait()


def place_of(j):
    return (j // 2) % XS, (j // 8) * PAIR + j % 2


def spread_kernel(where_ref, rank_ref, far_ref, hop_ref, own0_ref, far0_ref, next_ref, held_ref, out_ref):
    core = where_ref[0]
    z_own = where_ref[1]
    first_layer = where_ref[2] == 0

    @pl.when(core == 0)
    def _():
        for c in range(PAIR):
            own = jnp.where(first_layer, own0_ref[c], hop_ref[c])
            far = jnp.where(first_layer, far0_ref[c], far_ref[c])
            for z in range(2):
                block = jnp.where(z_own == z, own, far)
                for x in range(XS):
                    out_ref[x, z * PAIR + c] = block

    @pl.when(core == 1)
    def _():
        traces = []
        for c in range(PAIR):
            total = next_ref[c].astype(F32) + (hop_ref[c].astype(F32) + far_ref[c].astype(F32))
            traces.append(total.astype(BF))
        size = 16 // GROUPS
        coefs = {}
        for g in range(GROUPS + 1):
            for k in range(size):
                if g < GROUPS:
                    j = g * size + k
                    for n, row in ((0, 1), (1, 0)):
                        product = dot_rows(traces[row], held_ref[2 * n, j])
                        coefs[n, j] = coefficients(product, rank_ref[row, j])
                if g > 0:
                    j = (g - 1) * size + k
                    total = dot_cols(coefs[0, j], held_ref[1, j]) + dot_cols(coefs[1, j], held_ref[3, j])
                    x, slot = place_of(j)
                    out_ref[x, slot] = total.astype(BF)


def gather_kernel(where_ref, rank_ref, got_ref, next_ref, held_ref, far_ref, hop_ref):
    core = where_ref[0]
    z_own = where_ref[1]

    @pl.when(core == 0)
    def _():
        size = 16 // GROUPS
        coefs = {}
        totals = [next_ref[row].astype(F32) for row in range(PAIR)]
        for g in range(GROUPS + 1):
            for k in range(size):
                for row in range(PAIR):
                    if g < GROUPS:
                        j = g * size + k
                        x, slot = place_of(j)
                        product = dot_rows(got_ref[x, slot], held_ref[2 * row + 1, j])
                        coefs[row, j] = coefficients(product, rank_ref[row, j])
                    if g > 0:
                        j = (g - 1) * size + k
                        totals[row] = totals[row] + dot_cols(coefs[row, j], held_ref[2 * row, j])
        for row in range(PAIR):
            block = totals[row].astype(BF)
            hop_ref[row] = block
            far_ref[row] = block

    @pl.when(core == 1)
    def _():
        for c in range(PAIR):
            sums = []
            for z in range(2):
                total = got_ref[0, z * PAIR + c].astype(F32)
                for x in range(1, XS):
                    total = total + got_ref[x, z * PAIR + c].astype(F32)
                sums.append(total.astype(BF))
            hop_ref[c] = jnp.where(z_own == 0, sums[0], sums[1])
            far_ref[c] = jnp.where(z_own == 0, sums[1], sums[0])


def column(row, size):
    across = lax.broadcasted_iota(jnp.int32, (size, size), 1)
    along = lax.broadcasted_iota(jnp.int32, (size, size), 0)
    picked = jnp.where(across == along, jnp.broadcast_to(row, (size, size)), 0)
    return jnp.sum(picked, axis=1, keepdims=True)


def pack_kernel(layer_ref, source_ref, rank_ref, up_ref, down_ref, packed_ref):
    layer = layer_ref[0]
    width = packed_ref.shape[1]
    sources = jnp.broadcast_to(column(source_ref[...], HALF), (HALF, width))
    zero = jnp.zeros((HALF, width), BF)
    for part in range(2):
        packed_ref[pl.ds(part * HALF, HALF), :] = jnp.where(layer >= sources, up_ref[part], zero)
        packed_ref[pl.ds(ROWS + part * HALF, HALF), :] = jnp.where(layer <= sources, down_ref[part], zero)
    ranks = jnp.broadcast_to(column(rank_ref[...], 16), (16, width))
    packed_ref[pl.ds(2 * ROWS, 16), :] = ranks.astype(F32).astype(BF)


def call(kernel, outs, scalars, arrays):
    smem = pl.BlockSpec(memory_space=pltpu.SMEM)
    vmem = pl.BlockSpec(memory_space=pltpu.VMEM)
    arrays = [pltpu.with_memory_space_constraint(a, pltpu.VMEM) for a in arrays]
    return pl.pallas_call(
        kernel,
        out_shape=outs,
        in_specs=[smem] * len(scalars) + [vmem] * len(arrays),
        out_specs=jax.tree.map(lambda _: vmem, outs),
        compiler_params=pltpu.CompilerParams(vmem_limit_bytes=LIMIT),
        cost_estimate=pl.CostEstimate(flops=64 * 2 * 64 * 256 * 256, bytes_accessed=10 * 1024 * 1024, transcendentals=0),
    )(*scalars, *arrays)


def load(own, others):
    own = [pltpu.with_memory_space_constraint(f, pltpu.HBM) for f in own]
    return pl.pallas_call(
        load_kernel,
        out_shape=pltpu.VMEM((4,) + own[0].shape, BF),
        in_specs=[pl.BlockSpec(memory_space=pltpu.HBM)] * 2 + [pl.BlockSpec(memory_space=pl.ANY)] * 2,
        out_specs=pl.BlockSpec(memory_space=pltpu.VMEM),
        scratch_shapes=[pltpu.SemaphoreType.DMA((4,))],
        compiler_params=pltpu.CompilerParams(vmem_limit_bytes=LIMIT),
        cost_estimate=pl.CostEstimate(flops=0, bytes_accessed=8 * 1024 * 1024, transcendentals=0),
    )(*own, *others)


def on_device(layers, up_source, down_source, source_layer, u_factor, v_factor, block_rank):
    layer = lax.axis_index("gz")
    place = lax.axis_index("xy")
    core = place % 2
    z_own = place // 8
    both = ("gz", "xy")
    width = u_factor.shape[-1]
    max_rank = u_factor.shape[-2]
    step = max_rank // 4

    def send(block, target):
        route = []
        for l in range(layers):
            for i in range(16):
                to = target(l, i)
                if to is not None and 0 <= to[0] < layers:
                    route.append((l * 16 + i, to[0] * 16 + to[1]))
        return lax.ppermute(block, both, route)

    def ahead(l, i):
        return (l + 1, i) if i % 2 == 0 else (l - 1, i)

    def ahead_far(l, i):
        return (l + 1, i ^ 8) if i % 2 == 0 else (l - 1, i ^ 8)

    pairs = [[2 * k, 2 * k + 1] for k in range(8)]
    rings = [[block_of(x, z, c) for x in range(XS)] for z in range(2) for c in range(2)]

    vmem = pl.BlockSpec(memory_space=pltpu.VMEM)
    packed = pl.pallas_call(
        pack_kernel,
        out_shape=jax.ShapeDtypeStruct((2 * ROWS + 16, width), BF),
        in_specs=[pl.BlockSpec(memory_space=pltpu.SMEM)] + [vmem] * 4,
        out_specs=vmem,
    )(layer.astype(jnp.int32)[None], source_layer[None], block_rank[0], up_source[0], down_source[0])
    chip = lax.all_gather(packed, "xy", axis=0, axis_index_groups=pairs)
    mine = jnp.where(core == 0, chip[:, :ROWS], chip[:, ROWS : 2 * ROWS])
    limits = (chip[:, 2 * ROWS :, 0].astype(F32) * step).astype(jnp.int32)

    u_own = u_factor[0, 0].reshape(16, 2 * max_rank, width)
    v_own = v_factor[0, 0].reshape(16, 2 * max_rank, width)
    far0 = send(mine, lambda l, i: (l, i ^ 8) if i % 2 == 0 else None)
    following = send(mine, lambda l, i: (l - 1, i))
    u_other = lax.ppermute(u_own, "xy", [(i, i ^ 1) for i in range(16)])
    v_other = lax.ppermute(v_own, "xy", [(i, i ^ 1) for i in range(16)])

    where = jnp.stack([core, z_own, layer]).astype(jnp.int32)
    scalars = (where, limits)
    held = load((u_own, v_own), (u_other, v_other))
    pair_shape = jax.ShapeDtypeStruct((PAIR, ROWS, width), BF)
    ring_shape = jax.ShapeDtypeStruct((XS, 2 * PAIR, ROWS, width), BF)

    hop = jnp.where(core == 0, mine, jnp.zeros_like(mine))
    far = far0
    for sweep in range(STEPS):
        sent = call(spread_kernel, ring_shape, scalars, (far, hop, mine, far0, following, held))
        got = lax.all_to_all(sent, "xy", 0, 0, axis_index_groups=rings)
        away, near = call(gather_kernel, (pair_shape, pair_shape), scalars, (got, following, held))
        if sweep < STEPS - 1:
            far = send(away, ahead_far)
            hop = send(near, ahead)

    last = send(away, lambda l, i: (l + 1, i) if i % 2 == 0 else (l, i ^ 8))
    up_pair = jnp.where(layer == 0, mine, last)
    down_pair = (mine.astype(F32) + (near.astype(F32) + last.astype(F32))).astype(BF)
    final = jnp.where(core == 0, up_pair, down_pair)
    swapped = lax.all_gather(final[1 - core], "xy", axis=0, axis_index_groups=pairs)
    kept = final[core]
    other = swapped[1 - core]
    up_trace = jnp.where(core == 0, kept, other).reshape(up_source.shape)
    down_trace = jnp.where(core == 0, other, kept).reshape(up_source.shape)
    return up_trace, down_trace


def solution(mesh):
    in_specs = (
        P("gz", None, None, "xy"),
        P("gz", None, None, "xy"),
        P(),
        P("gz", "xy", None, None, None, None),
        P("gz", "xy", None, None, None, None),
        P("gz", "xy", None),
    )
    out_specs = (P("gz", None, None, "xy"), P("gz", None, None, "xy"))
    return jax.shard_map(
        functools.partial(on_device, mesh.shape["gz"]),
        mesh=mesh,
        in_specs=in_specs,
        out_specs=out_specs,
        check_vma=False,
    )
```

```python
import functools

import jax
import jax.numpy as jnp
from jax import lax
from jax.experimental import pallas as pl
from jax.experimental.pallas import tpu as pltpu
from jax.sharding import PartitionSpec as P

STEPS = 3
XS = 4
PAIR = 2
ROWS = 64
HALF = 32
GROUPS = 4
SIZE = 4
LIMIT = 16 * 1024 * 1024
BF = jnp.bfloat16
F32 = jnp.float32


def dot_rows(a, b):
    return lax.dot_general(a, b, (((1,), (1,)), ((), ())), preferred_element_type=F32)


def dot_cols(a, b):
    return lax.dot_general(a, b, (((1,), (0,)), ((), ())), preferred_element_type=F32)


def coefficients(product, limit):
    rank = product.shape[1] // 2
    real = product[:HALF, :rank] - product[HALF:, rank:]
    imag = product[:HALF, rank:] + product[HALF:, :rank]
    keep = lax.broadcasted_iota(jnp.int32, real.shape, 1) < limit
    real = jnp.where(keep, real, 0.0).astype(BF)
    imag = jnp.where(keep, imag, 0.0).astype(BF)
    top = jnp.concatenate([real, -imag], axis=1)
    bottom = jnp.concatenate([imag, real], axis=1)
    return jnp.concatenate([top, bottom], axis=0)


def block_of(x, z, c):
    return z * 8 + x * 2 + c


def load_kernel(u0, v0, u1, v1, held_ref, sems):
    copies = [pltpu.make_async_copy(ref, held_ref.at[n], sems.at[n]) for n, ref in enumerate((u0, v0, u1, v1))]
    for copy in copies:
        copy.start()
    for copy in copies:
        copy.wait()


def place_of(j):
    return (j // 2) % XS, (j // 8) * PAIR + j % 2


def added(*refs):
    total = refs[0].astype(F32)
    for ref in refs[1:]:
        total = total + ref.astype(F32)
    return total.astype(BF)


def spread(where_ref, rank_ref, own, far, down, held_ref, out_ref):
    core = where_ref[0]
    z_own = where_ref[1]

    @pl.when(core == 0)
    def _():
        for c in range(PAIR):
            near_block = own(c)
            far_block = far(c)
            for z in range(2):
                block = jnp.where(z_own == z, near_block, far_block)
                for x in range(XS):
                    out_ref[x, z * PAIR + c] = block

    @pl.when(core == 1)
    def _():
        traces = [down(c) for c in range(PAIR)]
        coefs = {}
        for g in range(GROUPS + 1):
            for k in range(SIZE):
                if g < GROUPS:
                    j = g * SIZE + k
                    for n in range(PAIR):
                        product = dot_rows(traces[1 - n], held_ref[2 * n, j])
                        coefs[n, j] = coefficients(product, rank_ref[1 - n, j])
                if g > 0:
                    j = (g - 1) * SIZE + k
                    total = dot_cols(coefs[0, j], held_ref[1, j]) + dot_cols(coefs[1, j], held_ref[3, j])
                    x, slot = place_of(j)
                    out_ref[x, slot] = total.astype(BF)


def first_spread_kernel(where_ref, rank_ref, own0_ref, far0_ref, next_ref, held_ref, out_ref):
    spread(
        where_ref,
        rank_ref,
        lambda c: own0_ref[c],
        lambda c: far0_ref[c],
        lambda c: next_ref[c],
        held_ref,
        out_ref,
    )


def spread_kernel(where_ref, rank_ref, far_ref, hop_ref, own0_ref, far0_ref, next_ref, held_ref, out_ref):
    spread(
        where_ref,
        rank_ref,
        lambda c: added(own0_ref[c], hop_ref[c]),
        lambda c: added(far0_ref[c], far_ref[c]),
        lambda c: added(next_ref[c], hop_ref[c], far_ref[c]),
        held_ref,
        out_ref,
    )


def gather_kernel(where_ref, rank_ref, got_ref, held_ref, far_ref, hop_ref):
    core = where_ref[0]
    z_own = where_ref[1]

    @pl.when(core == 0)
    def _():
        totals = [None, None]
        coefs = {}
        for g in range(GROUPS + 1):
            for k in range(SIZE):
                for row in range(PAIR):
                    if g < GROUPS:
                        j = g * SIZE + k
                        x, slot = place_of(j)
                        product = dot_rows(got_ref[x, slot], held_ref[2 * row + 1, j])
                        coefs[row, j] = coefficients(product, rank_ref[row, j])
                    if g > 0:
                        j = (g - 1) * SIZE + k
                        part = dot_cols(coefs[row, j], held_ref[2 * row, j])
                        totals[row] = part if totals[row] is None else totals[row] + part
        for row in range(PAIR):
            block = totals[row].astype(BF)
            hop_ref[row] = block
            far_ref[row] = block

    @pl.when(core == 1)
    def _():
        for c in range(PAIR):
            sums = []
            for z in range(2):
                total = got_ref[0, z * PAIR + c].astype(F32)
                for x in range(1, XS):
                    total = total + got_ref[x, z * PAIR + c].astype(F32)
                sums.append(total.astype(BF))
            hop_ref[c] = jnp.where(z_own == 0, sums[0], sums[1])
            far_ref[c] = jnp.where(z_own == 0, sums[1], sums[0])


def column(row, size):
    across = lax.broadcasted_iota(jnp.int32, (size, size), 1)
    along = lax.broadcasted_iota(jnp.int32, (size, size), 0)
    picked = jnp.where(across == along, jnp.broadcast_to(row, (size, size)), 0)
    return jnp.sum(picked, axis=1, keepdims=True)


def pack_kernel(layer_ref, source_ref, rank_ref, up_ref, down_ref, packed_ref):
    layer = layer_ref[0]
    width = packed_ref.shape[1]
    sources = jnp.broadcast_to(column(source_ref[...], HALF), (HALF, width))
    zero = jnp.zeros((HALF, width), BF)
    for part in range(2):
        packed_ref[pl.ds(part * HALF, HALF), :] = jnp.where(layer >= sources, up_ref[part], zero)
        packed_ref[pl.ds(ROWS + part * HALF, HALF), :] = jnp.where(layer <= sources, down_ref[part], zero)
    ranks = jnp.broadcast_to(column(rank_ref[...], 16), (16, width))
    packed_ref[pl.ds(2 * ROWS, 16), :] = ranks.astype(F32).astype(BF)


def call(kernel, outs, scalars, arrays):
    smem = pl.BlockSpec(memory_space=pltpu.SMEM)
    vmem = pl.BlockSpec(memory_space=pltpu.VMEM)
    arrays = [pltpu.with_memory_space_constraint(a, pltpu.VMEM) for a in arrays]
    return pl.pallas_call(
        kernel,
        out_shape=outs,
        in_specs=[smem] * len(scalars) + [vmem] * len(arrays),
        out_specs=jax.tree.map(lambda _: vmem, outs),
        compiler_params=pltpu.CompilerParams(vmem_limit_bytes=LIMIT),
        cost_estimate=pl.CostEstimate(flops=64 * 2 * 64 * 256 * 256, bytes_accessed=10 * 1024 * 1024, transcendentals=0),
    )(*scalars, *arrays)


def load(own, others):
    own = [pltpu.with_memory_space_constraint(f, pltpu.HBM) for f in own]
    return pl.pallas_call(
        load_kernel,
        out_shape=pltpu.VMEM((4,) + own[0].shape, BF),
        in_specs=[pl.BlockSpec(memory_space=pltpu.HBM)] * 2 + [pl.BlockSpec(memory_space=pl.ANY)] * 2,
        out_specs=pl.BlockSpec(memory_space=pltpu.VMEM),
        scratch_shapes=[pltpu.SemaphoreType.DMA((4,))],
        compiler_params=pltpu.CompilerParams(vmem_limit_bytes=LIMIT),
        cost_estimate=pl.CostEstimate(flops=0, bytes_accessed=8 * 1024 * 1024, transcendentals=0),
    )(*own, *others)


def on_device(layers, up_source, down_source, source_layer, u_factor, v_factor, block_rank):
    layer = lax.axis_index("gz")
    place = lax.axis_index("xy")
    core = place % 2
    z_own = place // 8
    both = ("gz", "xy")
    width = u_factor.shape[-1]
    max_rank = u_factor.shape[-2]
    step = max_rank // 4

    def send(block, target):
        route = []
        for l in range(layers):
            for i in range(16):
                to = target(l, i)
                if to is not None and 0 <= to[0] < layers:
                    route.append((l * 16 + i, to[0] * 16 + to[1]))
        return lax.ppermute(block, both, route)

    def ahead(l, i):
        return (l + 1, i) if i % 2 == 0 else (l - 1, i)

    def ahead_far(l, i):
        return (l + 1, i ^ 8) if i % 2 == 0 else (l - 1, i ^ 8)

    pairs = [[2 * k, 2 * k + 1] for k in range(8)]
    rings = [[block_of(x, z, c) for x in range(XS)] for z in range(2) for c in range(2)]

    vmem = pl.BlockSpec(memory_space=pltpu.VMEM)
    packed = pl.pallas_call(
        pack_kernel,
        out_shape=pltpu.VMEM((2 * ROWS + 16, width), BF),
        in_specs=[pl.BlockSpec(memory_space=pltpu.SMEM)] + [vmem] * 4,
        out_specs=vmem,
    )(layer.astype(jnp.int32)[None], source_layer[None], block_rank[0], up_source[0], down_source[0])
    chip = lax.all_gather(packed, "xy", axis=0, axis_index_groups=pairs)
    u_own = u_factor[0, 0].reshape(16, 2 * max_rank, width)
    v_own = v_factor[0, 0].reshape(16, 2 * max_rank, width)
    u_sent, v_sent, chip = lax.optimization_barrier((u_own, v_own, chip))
    u_other = lax.ppermute(u_sent, "xy", [(i, i ^ 1) for i in range(16)])
    v_other = lax.ppermute(v_sent, "xy", [(i, i ^ 1) for i in range(16)])
    mine = jnp.where(core == 0, chip[:, :ROWS], chip[:, ROWS : 2 * ROWS])
    limits = (chip[:, 2 * ROWS :, 0].astype(F32) * step).astype(jnp.int32)
    far0 = send(mine, lambda l, i: (l, i ^ 8) if i % 2 == 0 else None)
    following = send(mine, lambda l, i: (l - 1, i) if i % 2 == 1 else None)
    where = jnp.stack([core, z_own, layer]).astype(jnp.int32)
    scalars = (where, limits)
    held = load((u_own, v_own), (u_other, v_other))
    pair_shape = jax.ShapeDtypeStruct((PAIR, ROWS, width), BF)
    ring_shape = jax.ShapeDtypeStruct((XS, 2 * PAIR, ROWS, width), BF)

    for sweep in range(STEPS):
        if sweep == 0:
            sent = call(first_spread_kernel, ring_shape, scalars, (mine, far0, following, held))
        else:
            sent = call(spread_kernel, ring_shape, scalars, (far, hop, mine, far0, following, held))
        got = lax.all_to_all(sent, "xy", 0, 0, axis_index_groups=rings)
        away, near = call(gather_kernel, (pair_shape, pair_shape), scalars, (got, held))
        if sweep < STEPS - 1:
            far = send(away, ahead_far)
            hop = send(near, ahead)

    last = send(away, lambda l, i: (l + 1, i) if i % 2 == 0 else (l, i ^ 8))
    kept_sum = jnp.where(core == 0, jnp.zeros_like(near), near)
    final = (mine.astype(F32) + (kept_sum.astype(F32) + last.astype(F32))).astype(BF)
    swapped = lax.all_gather(final[1 - core], "xy", axis=0, axis_index_groups=pairs)
    kept = final[core]
    other = swapped[1 - core]
    up_trace = jnp.where(core == 0, kept, other).reshape(up_source.shape)
    down_trace = jnp.where(core == 0, other, kept).reshape(up_source.shape)
    return up_trace, down_trace


def solution(mesh):
    in_specs = (
        P("gz", None, None, "xy"),
        P("gz", None, None, "xy"),
        P(),
        P("gz", "xy", None, None, None, None),
        P("gz", "xy", None, None, None, None),
        P("gz", "xy", None),
    )
    out_specs = (P("gz", None, None, "xy"), P("gz", None, None, "xy"))
    return jax.shard_map(
        functools.partial(on_device, mesh.shape["gz"]),
        mesh=mesh,
        in_specs=in_specs,
        out_specs=out_specs,
        check_vma=False,
    )
```

```python
import functools

import jax
import jax.numpy as jnp
from jax import lax
from jax.experimental import pallas as pl
from jax.experimental.pallas import tpu as pltpu
from jax.sharding import PartitionSpec as P

STEPS = 3
XS = 4
PAIR = 2
ROWS = 64
HALF = 32
GROUPS = 4
SIZE = 4
LIMIT = 16 * 1024 * 1024
BF = jnp.bfloat16
F32 = jnp.float32


def dot_rows(a, b):
    return lax.dot_general(a, b, (((1,), (1,)), ((), ())), preferred_element_type=F32)


def dot_cols(a, b):
    return lax.dot_general(a, b, (((1,), (0,)), ((), ())), preferred_element_type=F32)


def my_place():
    place = lax.axis_index("xy")
    return lax.rem(place, 2), lax.div(place, 8)


def coefficients(product, limit):
    rank = product.shape[1] // 2
    real = product[:HALF, :rank] - product[HALF:, rank:]
    imag = product[:HALF, rank:] + product[HALF:, :rank]
    keep = lax.broadcasted_iota(jnp.int32, real.shape, 1) < jnp.broadcast_to(limit, real.shape)
    real = jnp.where(keep, real, 0.0).astype(BF)
    imag = jnp.where(keep, imag, 0.0).astype(BF)
    top = jnp.concatenate([real, -imag], axis=1)
    bottom = jnp.concatenate([imag, real], axis=1)
    return jnp.concatenate([top, bottom], axis=0)


def block_of(x, z, c):
    return z * 8 + x * 2 + c


def load_kernel(u0, v0, u1, v1, held_ref, sems):
    copies = [pltpu.make_async_copy(ref, held_ref.at[n], sems.at[n]) for n, ref in enumerate((u0, v0, u1, v1))]
    for copy in copies:
        copy.start()
    for copy in copies:
        copy.wait()


def place_of(j):
    return (j // 2) % XS, (j // 8) * PAIR + j % 2


def added(*refs):
    total = refs[0].astype(F32)
    for ref in refs[1:]:
        total = total + ref.astype(F32)
    return total.astype(BF)


def spread(rank_ref, own, far, down, held_ref, out_ref):
    core, z_own = my_place()

    @pl.when(core == 0)
    def _():
        for c in range(PAIR):
            near_block = own(c)
            far_block = far(c)
            for z in range(2):
                block = jnp.where(z_own == z, near_block, far_block)
                for x in range(XS):
                    out_ref[x, z * PAIR + c] = block

    @pl.when(core == 1)
    def _():
        traces = [down(c) for c in range(PAIR)]
        coefs = {}
        for g in range(GROUPS + 1):
            for k in range(SIZE):
                if g < GROUPS:
                    j = g * SIZE + k
                    for n in range(PAIR):
                        product = dot_rows(traces[1 - n], held_ref[2 * n, j])
                        coefs[n, j] = coefficients(product, rank_ref[pl.ds((1 - n) * 16 + j, 1), :])
                if g > 0:
                    j = (g - 1) * SIZE + k
                    total = dot_cols(coefs[0, j], held_ref[1, j]) + dot_cols(coefs[1, j], held_ref[3, j])
                    x, slot = place_of(j)
                    out_ref[x, slot] = total.astype(BF)


def first_spread_kernel(rank_ref, own0_ref, first_ref, held_ref, out_ref):
    spread(
        rank_ref,
        lambda c: own0_ref[c],
        lambda c: first_ref[c],
        lambda c: first_ref[c],
        held_ref,
        out_ref,
    )


def spread_kernel(rank_ref, far_ref, hop_ref, own0_ref, first_ref, held_ref, out_ref):
    spread(
        rank_ref,
        lambda c: added(own0_ref[c], hop_ref[c]),
        lambda c: added(first_ref[c], far_ref[c]),
        lambda c: added(first_ref[c], hop_ref[c], far_ref[c]),
        held_ref,
        out_ref,
    )


def gather_kernel(rank_ref, got_ref, held_ref, far_ref, hop_ref):
    core, z_own = my_place()

    @pl.when(core == 0)
    def _():
        totals = [None, None]
        coefs = {}
        for g in range(GROUPS + 1):
            for k in range(SIZE):
                for row in range(PAIR):
                    if g < GROUPS:
                        j = g * SIZE + k
                        x, slot = place_of(j)
                        product = dot_rows(got_ref[x, slot], held_ref[2 * row + 1, j])
                        coefs[row, j] = coefficients(product, rank_ref[pl.ds(row * 16 + j, 1), :])
                    if g > 0:
                        j = (g - 1) * SIZE + k
                        part = dot_cols(coefs[row, j], held_ref[2 * row, j])
                        totals[row] = part if totals[row] is None else totals[row] + part
        for row in range(PAIR):
            block = totals[row].astype(BF)
            hop_ref[row] = block
            far_ref[row] = block

    @pl.when(core == 1)
    def _():
        for c in range(PAIR):
            sums = []
            for z in range(2):
                total = got_ref[0, z * PAIR + c].astype(F32)
                for x in range(1, XS):
                    total = total + got_ref[x, z * PAIR + c].astype(F32)
                sums.append(total.astype(BF))
            hop_ref[c] = jnp.where(z_own == 0, sums[0], sums[1])
            far_ref[c] = jnp.where(z_own == 0, sums[1], sums[0])


def column(row, size):
    across = lax.broadcasted_iota(jnp.int32, (size, size), 1)
    along = lax.broadcasted_iota(jnp.int32, (size, size), 0)
    picked = jnp.where(across == along, jnp.broadcast_to(row, (size, size)), 0)
    return jnp.sum(picked, axis=1, keepdims=True)


def pack_kernel(layer_ref, source_ref, rank_ref, up_ref, down_ref, packed_ref):
    layer = layer_ref[0]
    width = packed_ref.shape[1]
    sources = jnp.broadcast_to(column(source_ref[...], HALF), (HALF, width))
    zero = jnp.zeros((HALF, width), BF)
    for part in range(2):
        packed_ref[pl.ds(part * HALF, HALF), :] = jnp.where(layer >= sources, up_ref[part], zero)
        packed_ref[pl.ds(ROWS + part * HALF, HALF), :] = jnp.where(layer <= sources, down_ref[part], zero)
    ranks = jnp.broadcast_to(column(rank_ref[...], 16), (16, width))
    packed_ref[pl.ds(2 * ROWS, 16), :] = ranks.astype(F32).astype(BF)


def call(kernel, outs, arrays):
    vmem = pl.BlockSpec(memory_space=pltpu.VMEM)
    arrays = [pltpu.with_memory_space_constraint(a, pltpu.VMEM) for a in arrays]
    return pl.pallas_call(
        kernel,
        out_shape=outs,
        in_specs=[vmem] * len(arrays),
        out_specs=jax.tree.map(lambda _: vmem, outs),
        compiler_params=pltpu.CompilerParams(vmem_limit_bytes=LIMIT),
        cost_estimate=pl.CostEstimate(flops=64 * 2 * 64 * 256 * 256, bytes_accessed=10 * 1024 * 1024, transcendentals=0),
    )(*arrays)


def load(own, others):
    own = [pltpu.with_memory_space_constraint(f, pltpu.HBM) for f in own]
    return pl.pallas_call(
        load_kernel,
        out_shape=pltpu.VMEM((4,) + own[0].shape, BF),
        in_specs=[pl.BlockSpec(memory_space=pltpu.HBM)] * 2 + [pl.BlockSpec(memory_space=pl.ANY)] * 2,
        out_specs=pl.BlockSpec(memory_space=pltpu.VMEM),
        scratch_shapes=[pltpu.SemaphoreType.DMA((4,))],
        compiler_params=pltpu.CompilerParams(vmem_limit_bytes=LIMIT),
        cost_estimate=pl.CostEstimate(flops=0, bytes_accessed=8 * 1024 * 1024, transcendentals=0),
    )(*own, *others)


def on_device(layers, up_source, down_source, source_layer, u_factor, v_factor, block_rank):
    layer = lax.axis_index("gz")
    place = lax.axis_index("xy")
    core = place % 2
    both = ("gz", "xy")
    width = u_factor.shape[-1]
    max_rank = u_factor.shape[-2]
    step = max_rank // 4

    def send(block, target):
        route = []
        for l in range(layers):
            for i in range(16):
                to = target(l, i)
                if to is not None and 0 <= to[0] < layers:
                    route.append((l * 16 + i, to[0] * 16 + to[1]))
        return lax.ppermute(block, both, route)

    def ahead(l, i):
        return (l + 1, i) if i % 2 == 0 else (l - 1, i)

    def ahead_far(l, i):
        return (l + 1, i ^ 8) if i % 2 == 0 else (l - 1, i ^ 8)

    pairs = [[2 * k, 2 * k + 1] for k in range(8)]
    rings = [[block_of(x, z, c) for x in range(XS)] for z in range(2) for c in range(2)]

    vmem = pl.BlockSpec(memory_space=pltpu.VMEM)
    packed = pl.pallas_call(
        pack_kernel,
        out_shape=pltpu.VMEM((2 * ROWS + 16, width), BF),
        in_specs=[pl.BlockSpec(memory_space=pltpu.SMEM)] + [vmem] * 4,
        out_specs=vmem,
    )(layer.astype(jnp.int32)[None], source_layer[None], block_rank[0], up_source[0], down_source[0])
    chip = lax.all_gather(packed, "xy", axis=0, axis_index_groups=pairs)
    u_own = u_factor[0, 0].reshape(16, 2 * max_rank, width)
    v_own = v_factor[0, 0].reshape(16, 2 * max_rank, width)
    u_sent, v_sent, chip = lax.optimization_barrier((u_own, v_own, chip))
    u_other = lax.ppermute(u_sent, "xy", [(i, i ^ 1) for i in range(16)])
    v_other = lax.ppermute(v_sent, "xy", [(i, i ^ 1) for i in range(16)])
    mine = jnp.where(core == 0, chip[:, :ROWS], chip[:, ROWS : 2 * ROWS])
    limits = (chip[:, 2 * ROWS :, :max_rank].astype(F32) * step).astype(jnp.int32).reshape(PAIR * 16, max_rank)
    first = send(mine, lambda l, i: (l, i ^ 8) if i % 2 == 0 else (l - 1, i))
    held = load((u_own, v_own), (u_other, v_other))
    pair_shape = jax.ShapeDtypeStruct((PAIR, ROWS, width), BF)
    ring_shape = jax.ShapeDtypeStruct((XS, 2 * PAIR, ROWS, width), BF)

    for sweep in range(STEPS):
        if sweep == 0:
            sent = call(first_spread_kernel, ring_shape, (limits, mine, first, held))
        else:
            sent = call(spread_kernel, ring_shape, (limits, far, hop, mine, first, held))
        got = lax.all_to_all(sent, "xy", 0, 0, axis_index_groups=rings)
        away, near = call(gather_kernel, (pair_shape, pair_shape), (limits, got, held))
        if sweep < STEPS - 1:
            far = send(away, ahead_far)
            hop = send(near, ahead)

    last = send(away, lambda l, i: (l + 1, i) if i % 2 == 0 else (l, i ^ 8))
    kept_sum = jnp.where(core == 0, jnp.zeros_like(near), near)
    final = (mine.astype(F32) + (kept_sum.astype(F32) + last.astype(F32))).astype(BF)
    swapped = lax.all_gather(final[1 - core], "xy", axis=0, axis_index_groups=pairs)
    kept = final[core]
    other = swapped[1 - core]
    up_trace = jnp.where(core == 0, kept, other).reshape(up_source.shape)
    down_trace = jnp.where(core == 0, other, kept).reshape(up_source.shape)
    return up_trace, down_trace


def solution(mesh):
    in_specs = (
        P("gz", None, None, "xy"),
        P("gz", None, None, "xy"),
        P(),
        P("gz", "xy", None, None, None, None),
        P("gz", "xy", None, None, None, None),
        P("gz", "xy", None),
    )
    out_specs = (P("gz", None, None, "xy"), P("gz", None, None, "xy"))
    return jax.shard_map(
        functools.partial(on_device, mesh.shape["gz"]),
        mesh=mesh,
        in_specs=in_specs,
        out_specs=out_specs,
        check_vma=False,
    )
```

```python
import functools

import jax
import jax.numpy as jnp
from jax import lax
from jax.experimental import pallas as pl
from jax.experimental.pallas import tpu as pltpu
from jax.sharding import PartitionSpec as P

STEPS = 3
XS = 4
PAIR = 2
ROWS = 64
HALF = 32
GROUPS = 4
SIZE = 4
LIMIT = 16 * 1024 * 1024
BF = jnp.bfloat16
F32 = jnp.float32


def dot_rows(a, b):
    return lax.dot_general(a, b, (((1,), (1,)), ((), ())), preferred_element_type=F32)


def dot_cols(a, b):
    return lax.dot_general(a, b, (((1,), (0,)), ((), ())), preferred_element_type=F32)


def my_place():
    place = lax.axis_index("xy")
    z_own = lax.div(place, 8)
    return lax.rem(place + z_own, 2), z_own


def coefficients(product, limit):
    rank = product.shape[1] // 2
    real = product[:HALF, :rank] - product[HALF:, rank:]
    imag = product[:HALF, rank:] + product[HALF:, :rank]
    keep = lax.broadcasted_iota(jnp.int32, real.shape, 1) < jnp.broadcast_to(limit, real.shape)
    real = jnp.where(keep, real, 0.0).astype(BF)
    imag = jnp.where(keep, imag, 0.0).astype(BF)
    top = jnp.concatenate([real, -imag], axis=1)
    bottom = jnp.concatenate([imag, real], axis=1)
    return jnp.concatenate([top, bottom], axis=0)


def block_of(x, z, c):
    return z * 8 + x * 2 + c


def load_kernel(u_own, v_own, u_other, v_other, held_ref, sems):
    own = 2 * lax.rem(lax.axis_index("xy"), 2)
    other = 2 - own
    copies = [
        pltpu.make_async_copy(ref, held_ref.at[slot], sems.at[n])
        for n, (ref, slot) in enumerate(((u_own, own), (v_own, own + 1), (u_other, other), (v_other, other + 1)))
    ]
    for copy in copies:
        copy.start()
    for copy in copies:
        copy.wait()


def place_of(j):
    return (j // 2) % XS, (j // 8) * PAIR + j % 2


def added(*refs):
    total = refs[0].astype(F32)
    for ref in refs[1:]:
        total = total + ref.astype(F32)
    return total.astype(BF)


def spread(rank_ref, own, far, down, held_ref, out_ref):
    role, z_own = my_place()

    @pl.when(role == 0)
    def _():
        for c in range(PAIR):
            near_block = own(c)
            far_block = far(c)
            for z in range(2):
                block = jnp.where(z_own == z, near_block, far_block)
                for x in range(XS):
                    out_ref[x, z * PAIR + c] = block

    @pl.when(role == 1)
    def _():
        traces = [down(c) for c in range(PAIR)]
        coefs = {}
        for g in range(GROUPS + 1):
            for k in range(SIZE):
                if g < GROUPS:
                    j = g * SIZE + k
                    for n in range(PAIR):
                        product = dot_rows(traces[n], held_ref[2 * n, j])
                        coefs[n, j] = coefficients(product, rank_ref[pl.ds(n * 16 + j, 1), :])
                if g > 0:
                    j = (g - 1) * SIZE + k
                    total = dot_cols(coefs[0, j], held_ref[1, j]) + dot_cols(coefs[1, j], held_ref[3, j])
                    x, slot = place_of(j)
                    out_ref[x, slot] = total.astype(BF)


def first_spread_kernel(rank_ref, own0_ref, first_ref, held_ref, out_ref):
    spread(
        rank_ref,
        lambda c: own0_ref[c],
        lambda c: first_ref[c],
        lambda c: first_ref[c],
        held_ref,
        out_ref,
    )


def spread_kernel(rank_ref, far_ref, hop_ref, own0_ref, first_ref, held_ref, out_ref):
    spread(
        rank_ref,
        lambda c: added(own0_ref[c], hop_ref[c]),
        lambda c: added(first_ref[c], far_ref[c]),
        lambda c: added(first_ref[c], hop_ref[c], far_ref[c]),
        held_ref,
        out_ref,
    )


def gather_kernel(rank_ref, got_ref, held_ref, far_ref, hop_ref):
    role, z_own = my_place()

    @pl.when(role == 0)
    def _():
        totals = [None, None]
        coefs = {}
        for g in range(GROUPS + 1):
            for k in range(SIZE):
                for row in range(PAIR):
                    if g < GROUPS:
                        j = g * SIZE + k
                        x, slot = place_of(j)
                        product = dot_rows(got_ref[x, slot], held_ref[2 * row + 1, j])
                        coefs[row, j] = coefficients(product, rank_ref[pl.ds(row * 16 + j, 1), :])
                    if g > 0:
                        j = (g - 1) * SIZE + k
                        part = dot_cols(coefs[row, j], held_ref[2 * row, j])
                        totals[row] = part if totals[row] is None else totals[row] + part
        for row in range(PAIR):
            block = totals[row].astype(BF)
            hop_ref[row] = block
            far_ref[row] = block

    @pl.when(role == 1)
    def _():
        for c in range(PAIR):
            sums = []
            for z in range(2):
                total = got_ref[0, z * PAIR + c].astype(F32)
                for x in range(1, XS):
                    total = total + got_ref[x, z * PAIR + c].astype(F32)
                sums.append(total.astype(BF))
            hop_ref[c] = jnp.where(z_own == 0, sums[0], sums[1])
            far_ref[c] = jnp.where(z_own == 0, sums[1], sums[0])


def column(row, size):
    across = lax.broadcasted_iota(jnp.int32, (size, size), 1)
    along = lax.broadcasted_iota(jnp.int32, (size, size), 0)
    picked = jnp.where(across == along, jnp.broadcast_to(row, (size, size)), 0)
    return jnp.sum(picked, axis=1, keepdims=True)


def pack_kernel(layer_ref, source_ref, rank_ref, up_ref, down_ref, packed_ref):
    layer = layer_ref[0]
    width = packed_ref.shape[1]
    sources = jnp.broadcast_to(column(source_ref[...], HALF), (HALF, width))
    zero = jnp.zeros((HALF, width), BF)
    for part in range(2):
        packed_ref[pl.ds(part * HALF, HALF), :] = jnp.where(layer >= sources, up_ref[part], zero)
        packed_ref[pl.ds(ROWS + part * HALF, HALF), :] = jnp.where(layer <= sources, down_ref[part], zero)
    ranks = jnp.broadcast_to(column(rank_ref[...], 16), (16, width))
    packed_ref[pl.ds(2 * ROWS, 16), :] = ranks.astype(F32).astype(BF)


def call(kernel, outs, arrays):
    vmem = pl.BlockSpec(memory_space=pltpu.VMEM)
    arrays = [pltpu.with_memory_space_constraint(a, pltpu.VMEM) for a in arrays]
    return pl.pallas_call(
        kernel,
        out_shape=outs,
        in_specs=[vmem] * len(arrays),
        out_specs=jax.tree.map(lambda _: vmem, outs),
        compiler_params=pltpu.CompilerParams(vmem_limit_bytes=LIMIT),
        cost_estimate=pl.CostEstimate(flops=64 * 2 * 64 * 256 * 256, bytes_accessed=10 * 1024 * 1024, transcendentals=0),
    )(*arrays)


def load(own, others):
    own = [pltpu.with_memory_space_constraint(f, pltpu.HBM) for f in own]
    return pl.pallas_call(
        load_kernel,
        out_shape=pltpu.VMEM((4,) + own[0].shape, BF),
        in_specs=[pl.BlockSpec(memory_space=pltpu.HBM)] * 2 + [pl.BlockSpec(memory_space=pl.ANY)] * 2,
        out_specs=pl.BlockSpec(memory_space=pltpu.VMEM),
        scratch_shapes=[pltpu.SemaphoreType.DMA((4,))],
        compiler_params=pltpu.CompilerParams(vmem_limit_bytes=LIMIT),
        cost_estimate=pl.CostEstimate(flops=0, bytes_accessed=8 * 1024 * 1024, transcendentals=0),
    )(*own, *others)


def on_device(layers, up_source, down_source, source_layer, u_factor, v_factor, block_rank):
    layer = lax.axis_index("gz")
    place = lax.axis_index("xy")
    core = place % 2
    up_here = (place + place // 8) % 2 == 0
    both = ("gz", "xy")
    width = u_factor.shape[-1]
    max_rank = u_factor.shape[-2]
    step = max_rank // 4

    def send(block, target):
        route = []
        for l in range(layers):
            for i in range(16):
                to = target(l, i)
                if to is not None and 0 <= to[0] < layers:
                    route.append((l * 16 + i, to[0] * 16 + to[1]))
        return lax.ppermute(block, both, route)

    def is_up(i):
        return (i + i // 8) % 2 == 0

    def far_of(l, i):
        return l, i ^ 9

    def ahead(l, i):
        return (l + 1, i) if is_up(i) else (l - 1, i)

    def ahead_far(l, i):
        return far_of(*ahead(l, i))

    pairs = [[2 * k, 2 * k + 1] for k in range(8)]
    rings = [[block_of(x, z, c) for x in range(XS)] for z in range(2) for c in range(2)]

    vmem = pl.BlockSpec(memory_space=pltpu.VMEM)
    packed = pl.pallas_call(
        pack_kernel,
        out_shape=pltpu.VMEM((2 * ROWS + 16, width), BF),
        in_specs=[pl.BlockSpec(memory_space=pltpu.SMEM)] + [vmem] * 4,
        out_specs=vmem,
    )(layer.astype(jnp.int32)[None], source_layer[None], block_rank[0], up_source[0], down_source[0])
    chip = lax.all_gather(packed, "xy", axis=0, axis_index_groups=pairs)
    u_own = u_factor[0, 0].reshape(16, 2 * max_rank, width)
    v_own = v_factor[0, 0].reshape(16, 2 * max_rank, width)
    u_sent, v_sent, chip = lax.optimization_barrier((u_own, v_own, chip))
    u_other = lax.ppermute(u_sent, "xy", [(i, i ^ 1) for i in range(16)])
    v_other = lax.ppermute(v_sent, "xy", [(i, i ^ 1) for i in range(16)])
    mine = jnp.where(up_here, chip[:, :ROWS], chip[:, ROWS : 2 * ROWS])
    limits = (chip[:, 2 * ROWS :, :max_rank].astype(F32) * step).astype(jnp.int32).reshape(PAIR * 16, max_rank)
    first = send(mine, lambda l, i: far_of(l, i) if is_up(i) else ahead(l, i))
    held = load((u_own, v_own), (u_other, v_other))
    pair_shape = jax.ShapeDtypeStruct((PAIR, ROWS, width), BF)
    ring_shape = jax.ShapeDtypeStruct((XS, 2 * PAIR, ROWS, width), BF)

    for sweep in range(STEPS):
        if sweep == 0:
            sent = call(first_spread_kernel, ring_shape, (limits, mine, first, held))
        else:
            sent = call(spread_kernel, ring_shape, (limits, far, hop, mine, first, held))
        got = lax.all_to_all(sent.reshape(XS * 2 * PAIR * ROWS, width), "xy", 0, 0, axis_index_groups=rings, tiled=True)
        got = got.reshape(sent.shape)
        away, near = call(gather_kernel, (pair_shape, pair_shape), (limits, got, held))
        if sweep < STEPS - 1:
            far = send(away, ahead_far)
            hop = send(near, ahead)

    last = send(away, lambda l, i: ahead(l, i) if is_up(i) else far_of(l, i))
    kept_sum = jnp.where(up_here, jnp.zeros_like(near), near)
    final = (mine.astype(F32) + (kept_sum.astype(F32) + last.astype(F32))).astype(BF)
    swapped = lax.all_gather(final[1 - core], "xy", axis=0, axis_index_groups=pairs)
    kept = final[core]
    other = swapped[1 - core]
    up_trace = jnp.where(up_here, kept, other).reshape(up_source.shape)
    down_trace = jnp.where(up_here, other, kept).reshape(up_source.shape)
    return up_trace, down_trace


def solution(mesh):
    in_specs = (
        P("gz", None, None, "xy"),
        P("gz", None, None, "xy"),
        P(),
        P("gz", "xy", None, None, None, None),
        P("gz", "xy", None, None, None, None),
        P("gz", "xy", None),
    )
    out_specs = (P("gz", None, None, "xy"), P("gz", None, None, "xy"))
    return jax.shard_map(
        functools.partial(on_device, mesh.shape["gz"]),
        mesh=mesh,
        in_specs=in_specs,
        out_specs=out_specs,
        check_vma=False,
    )
```

```python
import functools

import jax
import jax.numpy as jnp
from jax import lax
from jax.experimental import pallas as pl
from jax.experimental.pallas import tpu as pltpu
from jax.sharding import PartitionSpec as P

STEPS = 3
XS = 4
PAIR = 2
ROWS = 64
HALF = 32
GROUPS = 4
SIZE = 4
LIMIT = 16 * 1024 * 1024
BF = jnp.bfloat16
F32 = jnp.float32


def dot_rows(a, b):
    return lax.dot_general(a, b, (((1,), (1,)), ((), ())), preferred_element_type=F32)


def dot_cols(a, b):
    return lax.dot_general(a, b, (((1,), (0,)), ((), ())), preferred_element_type=F32)


def my_place():
    place = lax.axis_index("xy")
    z_own = lax.div(place, 8)
    return lax.rem(place + z_own, 2), z_own


def coefficients(product, limit):
    rank = product.shape[1] // 2
    real = product[:HALF, :rank] - product[HALF:, rank:]
    imag = product[:HALF, rank:] + product[HALF:, :rank]
    keep = lax.broadcasted_iota(jnp.int32, real.shape, 1) < jnp.broadcast_to(limit, real.shape)
    real = jnp.where(keep, real, 0.0).astype(BF)
    imag = jnp.where(keep, imag, 0.0).astype(BF)
    top = jnp.concatenate([real, -imag], axis=1)
    bottom = jnp.concatenate([imag, real], axis=1)
    return jnp.concatenate([top, bottom], axis=0)


def block_of(x, z, c):
    return z * 8 + x * 2 + c


def load_kernel(u_own, v_own, u_other, v_other, held_ref, sems):
    own = 2 * lax.rem(lax.axis_index("xy"), 2)
    other = 2 - own
    copies = [
        pltpu.make_async_copy(ref, held_ref.at[slot], sems.at[n])
        for n, (ref, slot) in enumerate(((u_own, own), (v_own, own + 1), (u_other, other), (v_other, other + 1)))
    ]
    for copy in copies:
        copy.start()
    for copy in copies:
        copy.wait()


def place_of(j):
    return (j // 2) % XS, (j // 8) * PAIR + j % 2


def added(*refs):
    total = refs[0].astype(F32)
    for ref in refs[1:]:
        total = total + ref.astype(F32)
    return total.astype(BF)


def spread(rank_ref, own, far, down, held_ref, out_ref):
    role, z_own = my_place()

    @pl.when(role == 0)
    def _():
        for c in range(PAIR):
            near_block = own(c)
            far_block = far(c)
            for z in range(2):
                block = jnp.where(z_own == z, near_block, far_block)
                for x in range(XS):
                    out_ref[x, z * PAIR + c] = block

    @pl.when(role == 1)
    def _():
        traces = [down(c) for c in range(PAIR)]
        coefs = {}
        for g in range(GROUPS + 1):
            for k in range(SIZE):
                if g < GROUPS:
                    j = g * SIZE + k
                    for n in range(PAIR):
                        product = dot_rows(traces[n], held_ref[2 * n, j])
                        coefs[n, j] = coefficients(product, rank_ref[pl.ds(n * 16 + j, 1), :])
                if g > 0:
                    j = (g - 1) * SIZE + k
                    total = dot_cols(coefs[0, j], held_ref[1, j]) + dot_cols(coefs[1, j], held_ref[3, j])
                    x, slot = place_of(j)
                    out_ref[x, slot] = total.astype(BF)


def first_spread_kernel(rank_ref, own0_ref, first_ref, held_ref, out_ref):
    spread(
        rank_ref,
        lambda c: own0_ref[c],
        lambda c: first_ref[c],
        lambda c: first_ref[c],
        held_ref,
        out_ref,
    )


def spread_kernel(rank_ref, far_ref, hop_ref, own0_ref, first_ref, held_ref, out_ref):
    spread(
        rank_ref,
        lambda c: added(own0_ref[c], hop_ref[c]),
        lambda c: added(first_ref[c], far_ref[c]),
        lambda c: added(first_ref[c], hop_ref[c], far_ref[c]),
        held_ref,
        out_ref,
    )


def gather_kernel(rank_ref, got_ref, held_ref, far_ref, hop_ref):
    role, z_own = my_place()

    @pl.when(role == 0)
    def _():
        totals = [None, None]
        coefs = {}
        for g in range(GROUPS + 1):
            for k in range(SIZE):
                for row in range(PAIR):
                    if g < GROUPS:
                        j = g * SIZE + k
                        x, slot = place_of(j)
                        product = dot_rows(got_ref[x, slot], held_ref[2 * row + 1, j])
                        coefs[row, j] = coefficients(product, rank_ref[pl.ds(row * 16 + j, 1), :])
                    if g > 0:
                        j = (g - 1) * SIZE + k
                        part = dot_cols(coefs[row, j], held_ref[2 * row, j])
                        totals[row] = part if totals[row] is None else totals[row] + part
        for row in range(PAIR):
            block = totals[row].astype(BF)
            hop_ref[row] = block
            far_ref[row] = block

    @pl.when(role == 1)
    def _():
        for c in range(PAIR):
            sums = []
            for z in range(2):
                total = got_ref[0, z * PAIR + c].astype(F32)
                for x in range(1, XS):
                    total = total + got_ref[x, z * PAIR + c].astype(F32)
                sums.append(total.astype(BF))
            hop_ref[c] = jnp.where(z_own == 0, sums[0], sums[1])
            far_ref[c] = jnp.where(z_own == 0, sums[1], sums[0])


def column(row, size):
    across = lax.broadcasted_iota(jnp.int32, (size, size), 1)
    along = lax.broadcasted_iota(jnp.int32, (size, size), 0)
    picked = jnp.where(across == along, jnp.broadcast_to(row, (size, size)), 0)
    return jnp.sum(picked, axis=1, keepdims=True)


def pack_kernel(source_ref, rank_ref, up_ref, down_ref, packed_ref):
    layer = lax.axis_index("gz")
    width = packed_ref.shape[1]
    sources = jnp.broadcast_to(column(source_ref[...], HALF), (HALF, width))
    zero = jnp.zeros((HALF, width), BF)
    for part in range(2):
        packed_ref[pl.ds(part * HALF, HALF), :] = jnp.where(layer >= sources, up_ref[part], zero)
        packed_ref[pl.ds(ROWS + part * HALF, HALF), :] = jnp.where(layer <= sources, down_ref[part], zero)
    ranks = jnp.broadcast_to(column(rank_ref[...], 16), (16, width))
    packed_ref[pl.ds(2 * ROWS, 16), :] = ranks.astype(F32).astype(BF)


def call(kernel, outs, arrays):
    vmem = pl.BlockSpec(memory_space=pltpu.VMEM)
    arrays = [pltpu.with_memory_space_constraint(a, pltpu.VMEM) for a in arrays]
    return pl.pallas_call(
        kernel,
        out_shape=outs,
        in_specs=[vmem] * len(arrays),
        out_specs=jax.tree.map(lambda _: vmem, outs),
        compiler_params=pltpu.CompilerParams(vmem_limit_bytes=LIMIT),
        cost_estimate=pl.CostEstimate(flops=64 * 2 * 64 * 256 * 256, bytes_accessed=10 * 1024 * 1024, transcendentals=0),
    )(*arrays)


def load(own, others):
    own = [pltpu.with_memory_space_constraint(f, pltpu.HBM) for f in own]
    return pl.pallas_call(
        load_kernel,
        out_shape=pltpu.VMEM((4,) + own[0].shape, BF),
        in_specs=[pl.BlockSpec(memory_space=pltpu.HBM)] * 2 + [pl.BlockSpec(memory_space=pl.ANY)] * 2,
        out_specs=pl.BlockSpec(memory_space=pltpu.VMEM),
        scratch_shapes=[pltpu.SemaphoreType.DMA((4,))],
        compiler_params=pltpu.CompilerParams(vmem_limit_bytes=LIMIT),
        cost_estimate=pl.CostEstimate(flops=0, bytes_accessed=8 * 1024 * 1024, transcendentals=0),
    )(*own, *others)


def on_device(layers, up_source, down_source, source_layer, u_factor, v_factor, block_rank):
    place = lax.axis_index("xy")
    core = place % 2
    up_here = (place + place // 8) % 2 == 0
    both = ("gz", "xy")
    width = u_factor.shape[-1]
    max_rank = u_factor.shape[-2]
    step = max_rank // 4

    def send(block, target):
        route = []
        for l in range(layers):
            for i in range(16):
                to = target(l, i)
                if to is not None and 0 <= to[0] < layers:
                    route.append((l * 16 + i, to[0] * 16 + to[1]))
        return lax.ppermute(block, both, route)

    def is_up(i):
        return (i + i // 8) % 2 == 0

    def far_of(l, i):
        return l, i ^ 9

    def ahead(l, i):
        return (l + 1, i) if is_up(i) else (l - 1, i)

    def ahead_far(l, i):
        return far_of(*ahead(l, i))

    pairs = [[2 * k, 2 * k + 1] for k in range(8)]
    rings = [[block_of(x, z, c) for x in range(XS)] for z in range(2) for c in range(2)]

    vmem = pl.BlockSpec(memory_space=pltpu.VMEM)
    packed = pl.pallas_call(
        pack_kernel,
        out_shape=pltpu.VMEM((2 * ROWS + 16, width), BF),
        in_specs=[vmem] * 4,
        out_specs=vmem,
    )(source_layer[None], block_rank[0], up_source[0], down_source[0])
    chip = lax.all_gather(packed, "xy", axis=0, axis_index_groups=pairs)
    u_own = u_factor[0, 0].reshape(16, 2 * max_rank, width)
    v_own = v_factor[0, 0].reshape(16, 2 * max_rank, width)
    u_sent, v_sent, chip = lax.optimization_barrier((u_own, v_own, chip))
    u_other = lax.ppermute(u_sent, "xy", [(i, i ^ 1) for i in range(16)])
    v_other = lax.ppermute(v_sent, "xy", [(i, i ^ 1) for i in range(16)])
    mine = jnp.where(up_here, chip[:, :ROWS], chip[:, ROWS : 2 * ROWS])
    limits = (chip[:, 2 * ROWS :, :max_rank].astype(F32) * step).astype(jnp.int32).reshape(PAIR * 16, max_rank)
    first = send(mine, lambda l, i: far_of(l, i) if is_up(i) else ahead(l, i))
    held = load((u_own, v_own), (u_other, v_other))
    pair_shape = jax.ShapeDtypeStruct((PAIR, ROWS, width), BF)
    ring_shape = jax.ShapeDtypeStruct((XS, 2 * PAIR, ROWS, width), BF)

    for sweep in range(STEPS):
        if sweep == 0:
            sent = call(first_spread_kernel, ring_shape, (limits, mine, first, held))
        else:
            sent = call(spread_kernel, ring_shape, (limits, far, hop, mine, first, held))
        got = lax.all_to_all(sent.reshape(XS * 2 * PAIR * ROWS, width), "xy", 0, 0, axis_index_groups=rings, tiled=True)
        got = got.reshape(sent.shape)
        away, near = call(gather_kernel, (pair_shape, pair_shape), (limits, got, held))
        if sweep < STEPS - 1:
            far = send(away, ahead_far)
            hop = send(near, ahead)

    last = send(away, lambda l, i: ahead(l, i) if is_up(i) else far_of(l, i))
    kept_sum = jnp.where(up_here, jnp.zeros_like(near), near)
    final = (mine.astype(F32) + (kept_sum.astype(F32) + last.astype(F32))).astype(BF)
    swapped = lax.all_gather(final[1 - core], "xy", axis=0, axis_index_groups=pairs)
    kept = final[core]
    other = swapped[1 - core]
    up_trace = jnp.where(up_here, kept, other).reshape(up_source.shape)
    down_trace = jnp.where(up_here, other, kept).reshape(up_source.shape)
    return up_trace, down_trace


def solution(mesh):
    in_specs = (
        P("gz", None, None, "xy"),
        P("gz", None, None, "xy"),
        P(),
        P("gz", "xy", None, None, None, None),
        P("gz", "xy", None, None, None, None),
        P("gz", "xy", None),
    )
    out_specs = (P("gz", None, None, "xy"), P("gz", None, None, "xy"))
    return jax.shard_map(
        functools.partial(on_device, mesh.shape["gz"]),
        mesh=mesh,
        in_specs=in_specs,
        out_specs=out_specs,
        check_vma=False,
    )
```
